32 devices in a mesh: seq: 16 (over z, y, x), tp: 2 (over core).
Axes of the slice: x: 2, y: 2, z: 4, core: 2. Of those that a mesh axis runs over, the one named last changes fastest.
Arguments:
- tokens: bfloat16 [2048, 4096], P('seq'), may hold values from -6 to 6
- w_query: bfloat16 [4096, 2048], P('seq', 'tp'), may hold values from -0.09375 to 0.09375
- w_key: bfloat16 [4096, 2048], P('seq', 'tp'), may hold values from -0.09375 to 0.09375
- w_value: bfloat16 [4096, 2048], P('seq', 'tp'), may hold values from -0.09375 to 0.09375
- short_taps: float32 [3, 3, 2048], P(None, None, 'tp'), may hold values from -2.5 to 2.5
- decay_rates: float32 [16, 2048], P(None, 'tp'), may hold values from 4.8828125e-05 to 0.04
- residues: float32 [16, 2048], P(None, 'tp'), may hold values from -1.2 to 1.2
- skip_gain: float32 [2048], P('tp'), may hold values from 0.5 to 1.5
- w_out: bfloat16 [2048, 4096], P('tp', 'seq'), may hold values from -0.125 to 0.125
Outputs:
- mixed: bfloat16 [2048, 4096], P('seq', 'tp')
The draws below stay inside these ranges and needn't reach their ends.
All inputs are finite; a program needn't handle non-finite values.
Results may differ from the reference program's by a relative error of at most 0.013.
Values may be sent and summed in bfloat16 or wider, within the bound.
No kernel may reach another device: no remote copies, remote signals or barrier semaphores. Data moves between devices by JAX's collectives and lax.ppermute only.
A program may use at most 128 MiB of HBM per device.

```python
import jax
import jax.numpy as jnp

D = 4096
C = 2048
ORDER = 16
SHORT = 3
SEQ_LEN = 2048


def modal_base(key):
    first_key, second_key = jax.random.split(key)
    spread = jax.random.uniform(first_key, (ORDER, C), jnp.float32)
    normals = jax.random.truncated_normal(second_key, -4.0, 4.0, (ORDER, C), jnp.float32)
    return (spread, normals)


def pick_rates(spread, lowest, highest):
    return jnp.exp(jnp.log(lowest) + spread * (jnp.log(highest) - jnp.log(lowest)))


def draw_decay_rates(key, part):
    spread, normals = modal_base(key)
    rates = pick_rates(spread, 0.3 / SEQ_LEN, 1.0 / 30.0)
    return rates


def draw_residues(key, part):
    spread, normals = modal_base(key)
    rates = pick_rates(spread, 0.3 / SEQ_LEN, 1.0 / 30.0)
    return normals * jnp.sqrt(2.0 * rates)


def block_scale(rng, shape, cuts, low, high):
    def one(position, parts):
        heights = jax.random.uniform(jax.random.fold_in(jax.random.fold_in(rng, 6), position), (parts,), jnp.float32, low / len(cuts), high / len(cuts))
        return jnp.repeat(jnp.exp(heights), shape[position] // parts).reshape((-1,) + (1,) * (len(shape) - position - 1))

    gain = one(*cuts[0])
    for cut in cuts[1:]:
        gain = gain * one(*cut)
    return gain


def scatter_about(own_key, dims, scale, limit, cuts=(), held_as=jnp.bfloat16):
    loudness = block_scale(own_key, dims, cuts, -0.22, 0.18) if cuts else 1.0
    drawn = jax.random.normal(own_key, dims, jnp.float32) * scale * loudness
    return jnp.minimum(jnp.maximum(drawn, -limit), limit).astype(held_as)


def setup_inputs(seed: int = 0) -> dict:
    splits = jax.random.split(jax.random.key(seed), 10)
    tokens = scatter_about(splits[0], (SEQ_LEN, D), 1.0, 6.0, ((0, 16),))
    w_query = scatter_about(splits[1], (D, C), D ** -0.5, 0.09375, ((0, 16), (1, 2)))
    w_key = scatter_about(splits[2], (D, C), D ** -0.5, 0.09375, ((0, 16), (1, 2)))
    w_value = scatter_about(splits[3], (D, C), D ** -0.5, 0.09375, ((0, 16), (1, 2)))
    short_taps = scatter_about(splits[4], (3, SHORT, C), 0.6, 2.5, ((2, 2),), jnp.float32)
    decay_rates = draw_decay_rates(jax.random.fold_in(splits[9], 71), 0)
    residues = draw_residues(jax.random.fold_in(splits[9], 71), 0)
    skip_gain = jnp.clip(0.5 + 1.0 * jax.random.uniform(splits[7], (C,), jnp.float32) ** block_scale(splits[7], (C,), ((0, 2),), -0.2, 0.2), 0.5, 1.5)
    w_out = scatter_about(splits[8], (C, D), C ** -0.5, 0.125, ((0, 2), (1, 16)))
    return {"tokens": tokens, "w_query": w_query, "w_key": w_key, "w_value": w_value, "short_taps": short_taps, "decay_rates": decay_rates, "residues": residues, "skip_gain": skip_gain, "w_out": w_out}


def short_filter(signal, taps):
    padded = jnp.pad(signal, ((SHORT - 1, 0), (0, 0)))
    result = jnp.zeros_like(signal)
    for lag in range(SHORT):
        result = result + taps[lag][None, :] * padded[SHORT - 1 - lag: SHORT - 1 - lag + SEQ_LEN]
    return result


def reference(tokens, w_query, w_key, w_value, short_taps, decay_rates, residues, skip_gain, w_out):
    query_proj = jnp.dot(tokens, w_query, preferred_element_type=jnp.float32)
    key_proj = jnp.dot(tokens, w_key, preferred_element_type=jnp.float32)
    value_proj = jnp.dot(tokens, w_value, preferred_element_type=jnp.float32)
    filt_q = short_filter(query_proj, short_taps[0])
    filt_k = short_filter(key_proj, short_taps[1])
    filt_v = short_filter(value_proj, short_taps[2])
    drive = filt_k * filt_v
    positions = jnp.arange(SEQ_LEN).astype(jnp.float32)[:, None]
    kernel = jnp.zeros((SEQ_LEN, C), jnp.float32)
    for mode in range(ORDER):
        kernel = kernel + residues[mode][None, :] * jnp.exp(-decay_rates[mode][None, :] * positions)
    length = 2 * SEQ_LEN
    spectrum = jnp.fft.rfft(drive, n=length, axis=0) * jnp.fft.rfft(kernel, n=length, axis=0)
    response = jnp.fft.irfft(spectrum, n=length, axis=0)[:SEQ_LEN] + skip_gain[None, :] * drive
    gated = (filt_q * response).astype(jnp.bfloat16)
    return jnp.dot(gated, w_out, preferred_element_type=jnp.float32).astype(jnp.bfloat16)
```

```python
import functools

import jax
import jax.numpy as jnp
from jax import lax
from jax.experimental import pallas as pl
from jax.experimental.pallas import tpu as pltpu
from jax.sharding import PartitionSpec as P

SHORT = 3
HALO = 8
SEGMENTS = 8
BF16 = jnp.bfloat16
F32 = jnp.float32


def flipped(value, axis, mask):
    size = lax.axis_size(axis)
    return lax.ppermute(value, axis, [(i, i ^ mask) for i in range(size)])


def spread(value, axis, count):
    return [value] + [flipped(value, axis, off) for off in range(1, count)]


def dot(left, right):
    return jnp.dot(left, right, preferred_element_type=F32)


def load_projected(g, padded, own, recv, halo, groups, rows):
    padded[0:HALO, :] = halo[...]
    for block in range(groups):
        source = lax.bitwise_xor(g, jnp.int32(block))
        start = HALO + block * rows
        padded[start : start + rows, :] = own[source] + recv[source].astype(F32)


def short_filter(padded, taps, start, rows):
    total = taps[0:1, :] * padded[HALO + start : HALO + start + rows, :]
    for lag in range(1, SHORT):
        first = HALO + start - lag
        total = total + taps[lag : lag + 1, :] * padded[first : first + rows, :]
    return total


def drive_kernel(
    groups, rows, order,
    g_ref, k_own, k_recv, k_halo, v_own, v_recv, v_halo, k_taps, v_taps, rates,
    drive, entry, last, k_pad, v_pad, ends,
):
    g = g_ref[0]
    load_projected(g, k_pad, k_own, k_recv, k_halo, groups, rows)
    load_projected(g, v_pad, v_own, v_recv, v_halo, groups, rows)
    length = groups * rows
    step_rows = min(64, rows)
    for start in range(0, length, step_rows):
        drive[start : start + step_rows, :] = short_filter(
            k_pad, k_taps, start, step_rows
        ) * short_filter(v_pad, v_taps, start, step_rows)
    segment = length // SEGMENTS
    lanes = drive.shape[1]
    factors = jnp.exp(-rates[...])
    wide = [jnp.broadcast_to(factors[j : j + 1, :], (SEGMENTS, lanes)) for j in range(order)]

    def step(t, states):
        now = drive[pl.ds(t, SEGMENTS, stride=segment), :]
        return tuple(s * f + now for s, f in zip(states, wide))

    zero = jnp.zeros((SEGMENTS, lanes), F32)
    states = lax.fori_loop(0, segment, step, (zero,) * order, unroll=8)
    for j in range(order):
        ends[j] = states[j]
    whole = jnp.exp(-rates[...] * float(segment))
    running = jnp.zeros((order, lanes), F32)
    for i in range(SEGMENTS):
        entry[i] = running
        running = running * whole + ends[:, i, :]
    last[...] = running


def gate_kernel(
    groups, rows, order,
    g_ref, drive, entry, before, q_own, q_recv, q_halo, q_taps, rates, residues, skip,
    gated, q_pad, begin, response,
):
    g = g_ref[0]
    length = groups * rows
    segment = length // SEGMENTS
    lanes = drive.shape[1]
    decay = rates[...]
    for i in range(SEGMENTS):
        begin[i] = entry[i] + jnp.exp(-decay * float(segment * i)) * before[...]
    factors = jnp.exp(-decay)
    weights = residues[...]
    wide = [jnp.broadcast_to(factors[j : j + 1, :], (SEGMENTS, lanes)) for j in range(order)]
    heavy = [jnp.broadcast_to(weights[j : j + 1, :], (SEGMENTS, lanes)) for j in range(order)]
    direct = jnp.broadcast_to(skip[...], (SEGMENTS, lanes))

    def step(t, states):
        now = drive[pl.ds(t, SEGMENTS, stride=segment), :]
        states = tuple(s * f + now for s, f in zip(states, wide))
        terms = [s * w for s, w in zip(states, heavy)] + [direct * now]
        while len(terms) > 1:
            terms = [sum(terms[i : i + 2]) for i in range(0, len(terms), 2)]
        response[pl.ds(t, SEGMENTS, stride=segment), :] = terms[0]
        return states

    first = tuple(begin[:, j, :] for j in range(order))
    lax.fori_loop(0, segment, step, first, unroll=4)
    load_projected(g, q_pad, q_own, q_recv, q_halo, groups, rows)
    step_rows = min(64, rows)
    for start in range(0, length, step_rows):
        value = short_filter(q_pad, q_taps, start, step_rows) * response[start : start + step_rows, :]
        gated[start : start + step_rows, :] = value.astype(BF16)


def by_lanes(shape, lanes):
    lead = len(shape) - 1
    return pl.BlockSpec((*shape[:-1], lanes), lambda i: (0,) * lead + (i,))


def call_by_lanes(kernel, lanes, args, outs, scratch, flops):
    width = outs[0].shape[-1]
    specs = [pl.BlockSpec(memory_space=pltpu.SMEM)] + [by_lanes(a.shape, lanes) for a in args[1:]]
    moved = sum(a.size * a.dtype.itemsize for a in [*args, *outs])
    return pl.pallas_call(
        kernel,
        grid=(width // lanes,),
        in_specs=specs,
        out_specs=[by_lanes(o.shape, lanes) for o in outs],
        out_shape=outs,
        scratch_shapes=scratch,
        compiler_params=pltpu.CompilerParams(vmem_limit_bytes=32 * 1024 * 1024),
        cost_estimate=pl.CostEstimate(flops=flops, bytes_accessed=moved, transcendentals=0),
    )(*args)


def body(tokens, w_query, w_key, w_value, short_taps, decay_rates, residues, skip_gain, w_out):
    seq_parts, tp_parts = lax.axis_size("seq"), lax.axis_size("tp")
    me, core = lax.axis_index("seq"), lax.axis_index("tp")
    rows, depth = tokens.shape
    order = decay_rates.shape[0]
    groups = seq_parts // 4
    low, high = groups, 2 * groups
    h, l, g = me // high, me // low % 2, me % groups
    width = w_query.shape[1] // groups
    half = depth // 2
    share = half // tp_parts
    length = groups * rows

    def at(side):
        return lax.dynamic_slice(tokens, (0, side * half + core * share), (rows, share))

    got = flipped(at(1 - h), "seq", high)
    layers = [[h_ * high + l_ * low + i for i in range(groups)] for h_ in range(2) for l_ in range(2)]

    def weight_of(w):
        blocks = w.reshape(w.shape[0], groups, width).transpose(1, 0, 2)
        mine = lax.all_to_all(blocks, "seq", 0, 0, axis_index_groups=layers)
        mine = mine.reshape(half // 2, width)
        theirs = flipped(mine, "seq", low)
        if tp_parts == 2:
            return [jnp.where((core ^ off) == l, mine, theirs) for off in range(2)]
        both = jnp.where(
            l == 0, jnp.concatenate([mine, theirs]), jnp.concatenate([theirs, mine])
        )
        return [
            lax.dynamic_slice(both, ((core ^ off) * share, 0), (share, width))
            for off in range(tp_parts)
        ]

    weights = {name: weight_of(w) for name, w in (("v", w_value), ("k", w_key), ("q", w_query))}

    def gathered(block):
        whole = jnp.concatenate(spread(block, "seq", groups))
        return spread(whole, "tp", tp_parts)

    there, here = gathered(got), gathered(at(h))

    def projected(name):
        theirs = sum(dot(t, w) for t, w in zip(there, weights[name]))
        mine = sum(dot(t, w) for t, w in zip(here, weights[name]))
        recv = flipped(theirs.astype(BF16), "seq", high)
        shape = (groups, rows, width)
        return mine.reshape(shape), theirs.reshape(shape), recv.reshape(shape)

    parts = {name: projected(name) for name in ("v", "k", "q")}

    def halo_of(names):
        last = (groups - 1) ^ g

        def tail(which):
            return jnp.concatenate(
                [
                    lax.dynamic_index_in_dim(parts[n][which], last, 0, False)[rows - HALO :]
                    for n in names
                ],
                axis=1,
            )

        mine, theirs = tail(0), tail(1)
        near = flipped(jnp.where(l == 0, mine, theirs), "seq", low)
        far = flipped(jnp.where(l == 0, theirs, mine), "seq", low | high)
        return jnp.where((h == 0) & (l == 0), 0.0, near + far)

    kv_halo, q_halo = halo_of(("k", "v")), halo_of(("q",))
    k_halo, v_halo = kv_halo[:, :width], kv_halo[:, width:]
    first = g * width

    def channels(value):
        return lax.dynamic_slice_in_dim(value, first, width, value.ndim - 1)

    taps, rates, heights = channels(short_taps), channels(decay_rates), channels(residues)
    skip = channels(skip_gain[None, :])
    lanes = min(128, width)
    g_in = g.astype(jnp.int32).reshape(1)
    padded = pltpu.VMEM((HALO + length, lanes), F32)
    drive, entry, last = call_by_lanes(
        functools.partial(drive_kernel, groups, rows, order),
        lanes,
        (
            g_in,
            parts["k"][0], parts["k"][2], k_halo,
            parts["v"][0], parts["v"][2], v_halo,
            taps[1], taps[2], rates,
        ),
        (
            jax.ShapeDtypeStruct((length, width), F32),
            jax.ShapeDtypeStruct((SEGMENTS, order, width), F32),
            jax.ShapeDtypeStruct((order, width), F32),
        ),
        [padded, padded, pltpu.VMEM((order, SEGMENTS, lanes), F32)],
        length * width * (2 * order + 16),
    )
    layer = 2 * h + l
    before = jnp.zeros_like(last)
    for flip in range(1, 4):
        other = layer ^ flip
        sent = flipped(last, "seq", flip * low)
        gap = jnp.maximum(layer - other - 1, 0).astype(F32) * float(length)
        before = before + jnp.where(other < layer, jnp.exp(-rates * gap) * sent, 0.0)
    (gated,) = call_by_lanes(
        functools.partial(gate_kernel, groups, rows, order),
        lanes,
        (
            g_in, drive, entry, before,
            parts["q"][0], parts["q"][2], q_halo,
            taps[0], rates, heights, skip,
        ),
        (jax.ShapeDtypeStruct((length, width), BF16),),
        [
            padded,
            pltpu.VMEM((SEGMENTS, order, lanes), F32),
            pltpu.VMEM((length, lanes), F32),
        ],
        length * width * (4 * order + 16),
    )
    gated = gated.reshape(groups, rows, width)
    if tp_parts != 2:
        mine = lax.all_to_all(gated, "seq", 0, 0, axis_index_groups=layers)
        mine = mine.transpose(1, 0, 2).reshape(rows, groups * width)
        columns = lax.all_gather(w_out, "seq", axis=1, tiled=True)
        partial_out = dot(mine, columns).astype(BF16)
        return lax.psum_scatter(partial_out, "tp", scatter_dimension=1, tiled=True)
    halves = [[h_ * high + i for i in range(high)] for h_ in range(2)]
    both = lax.all_to_all(
        jnp.concatenate([gated, gated]), "seq", 0, 0, axis_index_groups=halves
    )
    both = both.reshape(2, groups, rows, width).transpose(0, 2, 1, 3)
    both = both.reshape(2 * rows, groups * width)

    def columns_of(block, masks):
        held = block[None]
        for mask in masks:
            held = jnp.concatenate([held, flipped(held, "seq", mask)])
        return held

    bits = [1 << i for i in range(groups.bit_length() - 1)]
    block = w_out.shape[1]
    outs = []
    for source, masks in ((w_out, bits), (flipped(w_out, "seq", high), bits[::-1])):
        held = columns_of(source, masks)
        offs = [0]
        for mask in masks:
            offs = offs + [off ^ mask for off in offs]
        held = held.transpose(1, 0, 2).reshape(w_out.shape[0], groups * block)
        outs.append((dot(both, held).reshape(2 * rows, groups, block), offs))

    def in_order(value, offs):
        return jnp.concatenate(
            [
                lax.dynamic_index_in_dim(
                    value, jnp.asarray(offs, jnp.int32).argsort()[n ^ g], 1, False
                )
                for n in range(groups)
            ],
            axis=1,
        )

    own_out, other_out = (in_order(value, offs) for value, offs in outs)
    keep = jnp.where(h == core, own_out, other_out)
    give = jnp.where(h == core, other_out, own_out)
    summed = (keep + flipped(give.astype(BF16), "tp", 1).astype(F32)).astype(BF16)
    summed = summed.reshape(2, rows, groups * block)
    mine = lax.dynamic_index_in_dim(summed, l, 0, False)
    theirs = flipped(lax.dynamic_index_in_dim(summed, 1 - l, 0, False), "seq", low)
    return jnp.where(
        l == 0,
        jnp.concatenate([mine, theirs], axis=1),
        jnp.concatenate([theirs, mine], axis=1),
    )


def solution(mesh):
    in_specs = (
        P("seq", None),
        P("seq", "tp"),
        P("seq", "tp"),
        P("seq", "tp"),
        P(None, None, "tp"),
        P(None, "tp"),
        P(None, "tp"),
        P("tp"),
        P("tp", "seq"),
    )
    out_specs = P("seq", "tp")
    return jax.shard_map(body, mesh=mesh, in_specs=in_specs, out_specs=out_specs, check_vma=False)
```

```python
import functools

import jax
import jax.numpy as jnp
from jax import lax
from jax.experimental import pallas as pl
from jax.experimental.pallas import tpu as pltpu
from jax.sharding import PartitionSpec as P

SHORT = 3
HALO = 8
SEGMENTS = 8
BF16 = jnp.bfloat16
F32 = jnp.float32


def flipped(value, axis, mask):
    size = lax.axis_size(axis)
    return lax.ppermute(value, axis, [(i, i ^ mask) for i in range(size)])


def spread(value, axis, count):
    return [value] + [flipped(value, axis, off) for off in range(1, count)]


def swapped(blocks, groups):
    return lax.all_to_all(blocks, "seq", 0, 0, axis_index_groups=groups)


def after(value, *others):
    return lax.optimization_barrier((value, *others))[0]


def together(*values):
    return lax.optimization_barrier(values)


def in_order(blocks, g):
    count = len(blocks)
    ordered = []
    for n in range(count):
        block = blocks[n]
        for value in range(1, count):
            block = jnp.where(g == value, blocks[n ^ value], block)
        ordered.append(block)
    return ordered


def dot(left, right):
    return jnp.dot(left, right, preferred_element_type=F32)


def load_projected(g, padded, own, recv, halo, groups, rows):
    padded[0:HALO, :] = halo[...]
    for block in range(groups):
        source = lax.bitwise_xor(g, jnp.int32(block))
        start = HALO + block * rows
        padded[start : start + rows, :] = own[source] + recv[source].astype(F32)


def short_filter(padded, taps, start, rows):
    total = taps[0:1, :] * padded[HALO + start : HALO + start + rows, :]
    for lag in range(1, SHORT):
        first = HALO + start - lag
        total = total + taps[lag : lag + 1, :] * padded[first : first + rows, :]
    return total


def drive_kernel(
    groups, rows, order,
    g_ref, k_own, k_recv, k_halo, v_own, v_recv, v_halo, k_taps, v_taps, rates,
    drive, entry, last, k_pad, v_pad, ends,
):
    g = g_ref[0]
    load_projected(g, k_pad, k_own, k_recv, k_halo, groups, rows)
    load_projected(g, v_pad, v_own, v_recv, v_halo, groups, rows)
    length = groups * rows
    step_rows = min(64, rows)
    for start in range(0, length, step_rows):
        drive[start : start + step_rows, :] = short_filter(
            k_pad, k_taps, start, step_rows
        ) * short_filter(v_pad, v_taps, start, step_rows)
    segment = length // SEGMENTS
    lanes = drive.shape[1]
    factors = jnp.exp(-rates[...])
    wide = [jnp.broadcast_to(factors[j : j + 1, :], (SEGMENTS, lanes)) for j in range(order)]

    def step(t, states):
        now = drive[pl.ds(t, SEGMENTS, stride=segment), :]
        return tuple(s * f + now for s, f in zip(states, wide))

    zero = jnp.zeros((SEGMENTS, lanes), F32)
    states = lax.fori_loop(0, segment, step, (zero,) * order, unroll=8)
    for j in range(order):
        ends[j] = states[j]
    whole = jnp.exp(-rates[...] * float(segment))
    running = jnp.zeros((order, lanes), F32)
    for i in range(SEGMENTS):
        entry[i] = running
        running = running * whole + ends[:, i, :]
    last[...] = running


def gate_kernel(
    groups, rows, order,
    g_ref, drive, entry, before, q_own, q_recv, q_halo, q_taps, rates, residues, skip,
    gated, q_pad, begin, response,
):
    g = g_ref[0]
    length = groups * rows
    segment = length // SEGMENTS
    lanes = drive.shape[1]
    decay = rates[...]
    for i in range(SEGMENTS):
        begin[i] = entry[i] + jnp.exp(-decay * float(segment * i)) * before[...]
    factors = jnp.exp(-decay)
    weights = residues[...]
    wide = [jnp.broadcast_to(factors[j : j + 1, :], (SEGMENTS, lanes)) for j in range(order)]
    heavy = [jnp.broadcast_to(weights[j : j + 1, :], (SEGMENTS, lanes)) for j in range(order)]
    direct = jnp.broadcast_to(skip[...], (SEGMENTS, lanes))

    def step(t, states):
        now = drive[pl.ds(t, SEGMENTS, stride=segment), :]
        states = tuple(s * f + now for s, f in zip(states, wide))
        terms = [s * w for s, w in zip(states, heavy)] + [direct * now]
        while len(terms) > 1:
            terms = [sum(terms[i : i + 2]) for i in range(0, len(terms), 2)]
        response[pl.ds(t, SEGMENTS, stride=segment), :] = terms[0]
        return states

    first = tuple(begin[:, j, :] for j in range(order))
    lax.fori_loop(0, segment, step, first, unroll=4)
    load_projected(g, q_pad, q_own, q_recv, q_halo, groups, rows)
    step_rows = min(64, rows)
    for start in range(0, length, step_rows):
        value = short_filter(q_pad, q_taps, start, step_rows) * response[start : start + step_rows, :]
        gated[start : start + step_rows, :] = value.astype(BF16)


def by_lanes(shape, lanes):
    lead = len(shape) - 1
    return pl.BlockSpec((*shape[:-1], lanes), lambda i: (0,) * lead + (i,))


def call_by_lanes(kernel, lanes, args, outs, scratch, flops):
    width = outs[0].shape[-1]
    specs = [pl.BlockSpec(memory_space=pltpu.SMEM)] + [by_lanes(a.shape, lanes) for a in args[1:]]
    moved = sum(a.size * a.dtype.itemsize for a in [*args, *outs])
    return pl.pallas_call(
        kernel,
        grid=(width // lanes,),
        in_specs=specs,
        out_specs=[by_lanes(o.shape, lanes) for o in outs],
        out_shape=outs,
        scratch_shapes=scratch,
        compiler_params=pltpu.CompilerParams(vmem_limit_bytes=32 * 1024 * 1024),
        cost_estimate=pl.CostEstimate(flops=flops, bytes_accessed=moved, transcendentals=0),
    )(*args)


def body(tokens, w_query, w_key, w_value, short_taps, decay_rates, residues, skip_gain, w_out):
    seq_parts, tp_parts = lax.axis_size("seq"), lax.axis_size("tp")
    me, core = lax.axis_index("seq"), lax.axis_index("tp")
    rows, depth = tokens.shape
    order = decay_rates.shape[0]
    groups = seq_parts // 4
    low, high = groups, 2 * groups
    h, l, g = me // high, me // low % 2, me % groups
    width = w_query.shape[1] // groups
    half = depth // 2
    share = half // tp_parts
    length = groups * rows
    layers = [[layer * groups + i for i in range(groups)] for layer in range(4)]
    halves = [[side * high + i for i in range(high)] for side in range(2)]

    def at(side):
        return lax.dynamic_slice(tokens, (0, side * half + core * share), (rows, share))

    def block_of(w, off):
        return lax.dynamic_slice_in_dim(w, (g ^ off) * width, width, 1)

    def weight_of(mine, theirs):
        if tp_parts == 2:
            return [jnp.where((core ^ off) == l, mine, theirs) for off in range(2)]
        both = jnp.where(
            l == 0, jnp.concatenate([mine, theirs]), jnp.concatenate([theirs, mine])
        )
        return [
            lax.dynamic_slice(both, ((core ^ off) * share, 0), (share, mine.shape[1]))
            for off in range(tp_parts)
        ]

    def columns_of(block, masks):
        held, offs = block[None], [0]
        for mask in masks:
            held = jnp.concatenate([held, flipped(held, "seq", mask)])
            offs = offs + [off ^ mask for off in offs]
        ordered = in_order([held[offs.index(off)] for off in range(groups)], g)
        return jnp.concatenate(ordered, axis=1)

    got = flipped(at(1 - h), "seq", high)
    flat_vk = together(
        *(
            jnp.concatenate([block_of(w, off) for w in (w_value, w_key)], axis=1)
            for off in range(groups)
        )
    )
    flat_q = together(*(block_of(w_query, off) for off in range(groups)))

    def round_layer(blocks):
        return [blocks[0]] + [flipped(blocks[off], "seq", off) for off in range(1, groups)]

    came_vk, came_q = round_layer(flat_vk), round_layer(flat_q)
    out_depth = w_out.shape[0] // 2
    far_first = flipped(w_out[:out_depth], "seq", high)
    got, far_first, *came = together(got, far_first, *came_vk, *came_q)
    mine_vk = jnp.concatenate(in_order(came[:groups], g))
    mine_q = jnp.concatenate(in_order(came[groups:], g))

    def weight_of(mine, theirs):
        if tp_parts == 2:
            return [jnp.where((core ^ off) == l, mine, theirs) for off in range(2)]
        both = jnp.where(
            l == 0, jnp.concatenate([mine, theirs]), jnp.concatenate([theirs, mine])
        )
        return [
            lax.dynamic_slice(both, ((core ^ off) * share, 0), (share, mine.shape[1]))
            for off in range(tp_parts)
        ]

    def columns_of(block, masks):
        held, offs = block[None], [0]
        for mask in masks:
            held = jnp.concatenate([held, flipped(held, "seq", mask)])
            offs = offs + [off ^ mask for off in offs]
        ordered = in_order([held[offs.index(off)] for off in range(groups)], g)
        return jnp.concatenate(ordered, axis=1)

    got = flipped(at(1 - h), "seq", high)
    flat = together(
        *(
            jnp.concatenate([block_of(w, off) for w in (w_value, w_key, w_query)], axis=1)
            for off in range(groups)
        )
    )
    came = [flat[0]] + [flipped(flat[off], "seq", off) for off in range(1, groups)]
    out_depth = w_out.shape[0] // 2
    far_first = flipped(w_out[:out_depth], "seq", high)

    theirs_vk = flipped(mine_vk, "seq", low)
    far_last = flipped(after(w_out[out_depth:], got), "seq", high)
    *there, far_last = together(*spread(got, "seq", groups), far_last)
    here = spread(after(at(h), there[0]), "seq", groups)
    there = spread(jnp.concatenate(there), "tp", tp_parts)
    theirs_vk, mine_q, *both = together(theirs_vk, mine_q, *there, *here)
    there, here = both[:tp_parts], both[tp_parts:]

    def partial_sums(shares, weights):
        return sum(dot(t, w) for t, w in zip(shares, weights))

    def sent_over(value):
        return flipped(value.astype(BF16), "seq", high)

    def rows_before(mine, theirs):
        last = (groups - 1) ^ g

        def tail(value):
            value = value.reshape(groups, rows, -1)
            return lax.dynamic_index_in_dim(value, last, 0, False)[rows - HALO :]

        mine, theirs = tail(mine), tail(theirs)
        near = flipped(jnp.where(l == 0, mine, theirs), "seq", low)
        far = flipped(jnp.where(l == 0, theirs, mine), "seq", low | high)
        return jnp.where((h == 0) & (l == 0), 0.0, near + far)

    weights_vk = weight_of(mine_vk, theirs_vk)
    there_vk = partial_sums(there, weights_vk)
    recv_vk = sent_over(there_vk)
    here = spread(jnp.concatenate(here), "tp", tp_parts)
    theirs_q = flipped(after(mine_q, there_vk), "seq", low)
    here_vk = partial_sums(here, weights_vk)
    vk_halo = rows_before(here_vk, there_vk)
    recv_vk, theirs_q, vk_halo, *here = together(recv_vk, theirs_q, vk_halo, *here)

    weights_q = weight_of(mine_q, theirs_q)
    there_q = partial_sums(there, weights_q)
    recv_q = sent_over(there_q)
    here_q = partial_sums(here, weights_q)
    q_halo = rows_before(here_q, there_q)

    def named(vk, q):
        shape = (groups, rows, width)
        return {"v": vk[:, :width].reshape(shape), "k": vk[:, width:].reshape(shape), "q": q.reshape(shape)}

    here_parts, recv_parts = named(here_vk, here_q), named(recv_vk, recv_q)
    parts = {n: (here_parts[n], None, recv_parts[n]) for n in ("v", "k", "q")}
    v_halo, k_halo = vk_halo[:, :width], vk_halo[:, width:]

    def channels(value):
        return lax.dynamic_slice_in_dim(value, g * width, width, value.ndim - 1)

    taps, rates, heights = channels(short_taps), channels(decay_rates), channels(residues)
    skip = channels(skip_gain[None, :])
    lanes = min(128, width)
    g_in = g.astype(jnp.int32).reshape(1)
    padded = pltpu.VMEM((HALO + length, lanes), F32)
    drive, entry, last = call_by_lanes(
        functools.partial(drive_kernel, groups, rows, order),
        lanes,
        (
            g_in,
            parts["k"][0], parts["k"][2], k_halo,
            parts["v"][0], parts["v"][2], v_halo,
            taps[1], taps[2], rates,
        ),
        (
            jax.ShapeDtypeStruct((length, width), F32),
            jax.ShapeDtypeStruct((SEGMENTS, order, width), F32),
            jax.ShapeDtypeStruct((order, width), F32),
        ),
        [padded, padded, pltpu.VMEM((order, SEGMENTS, lanes), F32)],
        length * width * (2 * order + 16),
    )
    if tp_parts == 2:
        bits = [1 << i for i in range(groups.bit_length() - 1)]
        own_columns = columns_of(after(w_out, there_vk), bits)
        far_columns = columns_of(after(jnp.concatenate([far_first, far_last]), there_vk), bits[::-1])
        keep_columns = jnp.where(h == core, own_columns, far_columns)
        give_columns = jnp.where(h == core, far_columns, own_columns)
        before_gate = (keep_columns, give_columns)
    layer = 2 * h + l
    before = jnp.zeros_like(last)
    for flip in range(1, 4):
        other = layer ^ flip
        sent = flipped(last, "seq", flip * low)
        gap = jnp.maximum(layer - other - 1, 0).astype(F32) * float(length)
        before = before + jnp.where(other < layer, jnp.exp(-rates * gap) * sent, 0.0)
    if tp_parts == 2:
        before, keep_columns, give_columns = together(before, *before_gate)
    (gated,) = call_by_lanes(
        functools.partial(gate_kernel, groups, rows, order),
        lanes,
        (
            g_in, drive, entry, before,
            parts["q"][0], parts["q"][2], q_halo,
            taps[0], rates, heights, skip,
        ),
        (jax.ShapeDtypeStruct((length, width), BF16),),
        [
            padded,
            pltpu.VMEM((SEGMENTS, order, lanes), F32),
            pltpu.VMEM((length, lanes), F32),
        ],
        length * width * (4 * order + 16),
    )
    gated = gated.reshape(groups, rows, width)
    if tp_parts != 2:
        mine = swapped(gated, layers).transpose(1, 0, 2).reshape(rows, groups * width)
        columns = lax.all_gather(w_out, "seq", axis=1, tiled=True)
        partial_out = dot(mine, columns).astype(BF16)
        return lax.psum_scatter(partial_out, "tp", scatter_dimension=1, tiled=True)

    both = swapped(
        jnp.concatenate([gated, gated]), halves
    )
    both = both.reshape(2, groups, rows, width).transpose(0, 2, 1, 3)
    both = both.reshape(2 * rows, groups * width)
    give = dot(both, give_columns).astype(BF16)
    keep = dot(both, keep_columns)
    summed = (keep + flipped(give, "tp", 1).astype(F32)).astype(BF16)
    summed = summed.reshape(2, rows, -1)
    ours = lax.dynamic_index_in_dim(summed, l, 0, False)
    theirs = flipped(lax.dynamic_index_in_dim(summed, 1 - l, 0, False), "seq", low)
    return jnp.where(
        l == 0,
        jnp.concatenate([ours, theirs], axis=1),
        jnp.concatenate([theirs, ours], axis=1),
    )


def solution(mesh):
    in_specs = (
        P("seq", None),
        P("seq", "tp"),
        P("seq", "tp"),
        P("seq", "tp"),
        P(None, None, "tp"),
        P(None, "tp"),
        P(None, "tp"),
        P("tp"),
        P("tp", "seq"),
    )
    out_specs = P("seq", "tp")
    return jax.shard_map(body, mesh=mesh, in_specs=in_specs, out_specs=out_specs, check_vma=False)
```

```python
import functools

import jax
import jax.numpy as jnp
from jax import lax
from jax.experimental import pallas as pl
from jax.experimental.pallas import tpu as pltpu
from jax.sharding import PartitionSpec as P

SHORT = 3
HALO = 8
SEGMENTS = 8
BF16 = jnp.bfloat16
F32 = jnp.float32


def flipped(value, axis, mask):
    size = lax.axis_size(axis)
    return lax.ppermute(value, axis, [(i, i ^ mask) for i in range(size)])


def spread(value, axis, count):
    return [value] + [flipped(value, axis, off) for off in range(1, count)]


def swapped(blocks, groups):
    return lax.all_to_all(blocks, "seq", 0, 0, axis_index_groups=groups)


def after(value, *others):
    return lax.optimization_barrier((value, *others))[0]


def together(*values):
    return lax.optimization_barrier(values)


def in_order(blocks, g):
    count = len(blocks)
    ordered = []
    for n in range(count):
        block = blocks[n]
        for value in range(1, count):
            block = jnp.where(g == value, blocks[n ^ value], block)
        ordered.append(block)
    return ordered


def dot(left, right):
    return jnp.dot(left, right, preferred_element_type=F32)


def load_projected(g, padded, own, recv, halo, groups, rows):
    padded[0:HALO, :] = halo[...]
    for block in range(groups):
        source = lax.bitwise_xor(g, jnp.int32(block))
        start = HALO + block * rows
        padded[start : start + rows, :] = own[source] + recv[source].astype(F32)


def short_filter(padded, taps, start, rows):
    total = taps[0:1, :] * padded[HALO + start : HALO + start + rows, :]
    for lag in range(1, SHORT):
        first = HALO + start - lag
        total = total + taps[lag : lag + 1, :] * padded[first : first + rows, :]
    return total


def drive_kernel(
    groups, rows, order,
    g_ref, k_own, k_recv, k_halo, v_own, v_recv, v_halo, k_taps, v_taps, rates,
    drive, entry, last, k_pad, v_pad, ends,
):
    g = g_ref[0]
    load_projected(g, k_pad, k_own, k_recv, k_halo, groups, rows)
    load_projected(g, v_pad, v_own, v_recv, v_halo, groups, rows)
    length = groups * rows
    step_rows = min(64, rows)
    for start in range(0, length, step_rows):
        drive[start : start + step_rows, :] = short_filter(
            k_pad, k_taps, start, step_rows
        ) * short_filter(v_pad, v_taps, start, step_rows)
    segment = length // SEGMENTS
    lanes = drive.shape[1]
    factors = jnp.exp(-rates[...])
    wide = [jnp.broadcast_to(factors[j : j + 1, :], (SEGMENTS, lanes)) for j in range(order)]

    def step(t, states):
        now = drive[pl.ds(t, SEGMENTS, stride=segment), :]
        return tuple(s * f + now for s, f in zip(states, wide))

    zero = jnp.zeros((SEGMENTS, lanes), F32)
    states = lax.fori_loop(0, segment, step, (zero,) * order, unroll=8)
    for j in range(order):
        ends[j] = states[j]
    whole = jnp.exp(-rates[...] * float(segment))
    running = jnp.zeros((order, lanes), F32)
    for i in range(SEGMENTS):
        entry[i] = running
        running = running * whole + ends[:, i, :]
    last[...] = running


def gate_kernel(
    groups, rows, order,
    g_ref, drive, entry, before, q_own, q_recv, q_halo, q_taps, rates, residues, skip,
    gated, q_pad, begin, response,
):
    g = g_ref[0]
    length = groups * rows
    segment = length // SEGMENTS
    lanes = drive.shape[1]
    decay = rates[...]
    for i in range(SEGMENTS):
        begin[i] = entry[i] + jnp.exp(-decay * float(segment * i)) * before[...]
    factors = jnp.exp(-decay)
    weights = residues[...]
    wide = [jnp.broadcast_to(factors[j : j + 1, :], (SEGMENTS, lanes)) for j in range(order)]
    heavy = [jnp.broadcast_to(weights[j : j + 1, :], (SEGMENTS, lanes)) for j in range(order)]
    direct = jnp.broadcast_to(skip[...], (SEGMENTS, lanes))

    def step(t, states):
        now = drive[pl.ds(t, SEGMENTS, stride=segment), :]
        states = tuple(s * f + now for s, f in zip(states, wide))
        terms = [s * w for s, w in zip(states, heavy)] + [direct * now]
        while len(terms) > 1:
            terms = [sum(terms[i : i + 2]) for i in range(0, len(terms), 2)]
        response[pl.ds(t, SEGMENTS, stride=segment), :] = terms[0]
        return states

    first = tuple(begin[:, j, :] for j in range(order))
    lax.fori_loop(0, segment, step, first, unroll=4)
    load_projected(g, q_pad, q_own, q_recv, q_halo, groups, rows)
    step_rows = min(64, rows)
    for start in range(0, length, step_rows):
        value = short_filter(q_pad, q_taps, start, step_rows) * response[start : start + step_rows, :]
        gated[start : start + step_rows, :] = value.astype(BF16)


def assemble_kernel(depth, cuts, place, *refs):
    count = len(refs) - len(cuts)
    for off in range(count):
        start = pl.multiple_of(lax.bitwise_xor(place[0], jnp.int32(off)) * depth, depth)
        for (first, last), out in zip(cuts, refs[count:]):
            out[pl.ds(start, depth), :] = refs[off][:, first:last]


def assemble(place, blocks, cuts):
    depth = blocks[0].shape[0]
    outs = [jax.ShapeDtypeStruct((len(blocks) * depth, last - first), BF16) for first, last in cuts]
    return pl.pallas_call(
        functools.partial(assemble_kernel, depth, cuts),
        in_specs=[pl.BlockSpec(memory_space=pltpu.SMEM)]
        + [pl.BlockSpec(memory_space=pltpu.VMEM)] * len(blocks),
        out_specs=[pl.BlockSpec(memory_space=pltpu.VMEM)] * len(outs),
        out_shape=outs,
        compiler_params=pltpu.CompilerParams(vmem_limit_bytes=32 * 1024 * 1024),
        cost_estimate=pl.CostEstimate(
            flops=0, bytes_accessed=sum(a.size * 2 for a in [*blocks, *outs]), transcendentals=0
        ),
    )(place, *blocks)


def by_lanes(shape, lanes):
    lead = len(shape) - 1
    return pl.BlockSpec((*shape[:-1], lanes), lambda i: (0,) * lead + (i,))


def call_by_lanes(kernel, lanes, args, outs, scratch, flops):
    width = outs[0].shape[-1]
    specs = [pl.BlockSpec(memory_space=pltpu.SMEM)] + [by_lanes(a.shape, lanes) for a in args[1:]]
    moved = sum(a.size * a.dtype.itemsize for a in [*args, *outs])
    return pl.pallas_call(
        kernel,
        grid=(width // lanes,),
        in_specs=specs,
        out_specs=[by_lanes(o.shape, lanes) for o in outs],
        out_shape=outs,
        scratch_shapes=scratch,
        compiler_params=pltpu.CompilerParams(vmem_limit_bytes=32 * 1024 * 1024),
        cost_estimate=pl.CostEstimate(flops=flops, bytes_accessed=moved, transcendentals=0),
    )(*args)


def body(tokens, w_query, w_key, w_value, short_taps, decay_rates, residues, skip_gain, w_out):
    seq_parts, tp_parts = lax.axis_size("seq"), lax.axis_size("tp")
    me, core = lax.axis_index("seq"), lax.axis_index("tp")
    rows, depth = tokens.shape
    order = decay_rates.shape[0]
    groups = seq_parts // 4
    low, high = groups, 2 * groups
    h, l, g = me // high, me // low % 2, me % groups
    width = w_query.shape[1] // groups
    half = depth // 2
    share = half // tp_parts
    length = groups * rows
    layers = [[layer * groups + i for i in range(groups)] for layer in range(4)]
    halves = [[side * high + i for i in range(high)] for side in range(2)]
    g_in = g.astype(jnp.int32).reshape(1)

    def at(side):
        return lax.dynamic_slice(tokens, (0, side * half + core * share), (rows, share))

    def block_of(w, off):
        return lax.dynamic_slice_in_dim(w, (g ^ off) * width, width, 1)

    def channels(value):
        return lax.dynamic_slice_in_dim(value, g * width, width, value.ndim - 1)

    def weight_of(mine, theirs):
        if tp_parts == 2:
            return [jnp.where((core ^ off) == l, mine, theirs) for off in range(2)]
        both = jnp.where(
            l == 0, jnp.concatenate([mine, theirs]), jnp.concatenate([theirs, mine])
        )
        return [
            lax.dynamic_slice(both, ((core ^ off) * share, 0), (share, mine.shape[1]))
            for off in range(tp_parts)
        ]

    def partial_sums(shares, weights):
        return sum(dot(t, w) for t, w in zip(shares, weights))

    def sent_over(value):
        return flipped(value.astype(BF16), "seq", high)

    def rows_before(mine, theirs):
        last = (groups - 1) ^ g

        def tail(value):
            value = value.reshape(groups, rows, -1)
            return lax.dynamic_index_in_dim(value, last, 0, False)[rows - HALO :]

        mine, theirs = tail(mine), tail(theirs)
        return jnp.where(l == 0, mine, theirs), jnp.where(l == 0, theirs, mine)

    def halo_of(near, far):
        return jnp.where((h == 0) & (l == 0), 0.0, near + far)

    given = at(1 - h)
    got = flipped(given, "seq", high)
    all_weights = [after(w, given) for w in (w_value, w_key, w_query)]
    flat = together(
        *(
            jnp.concatenate([block_of(w, off) for w in all_weights], axis=1)
            for off in range(groups)
        )
    )
    came = [flat[0]] + [flipped(flat[off], "seq", off) for off in range(1, groups)]
    out_depth = w_out.shape[0] // 2
    far_first = flipped(w_out[:out_depth], "seq", high)
    got, far_first, taps, rates, heights, skip, *came = together(
        got, far_first, channels(short_taps), channels(decay_rates), channels(residues),
        channels(skip_gain[None, :]), *came,
    )
    cuts = ((0, 2 * width), (2 * width, 3 * width))
    if width % 128 == 0 and w_query.shape[0] % 16 == 0:
        mine_vk, mine_q = assemble(g_in, came, cuts)
    else:
        whole = jnp.concatenate(in_order(came, g))
        mine_vk, mine_q = (whole[:, first:last] for first, last in cuts)

    theirs_vk = flipped(mine_vk, "seq", low)
    far_last = flipped(after(w_out[out_depth:], got), "seq", high)
    there = spread(got, "seq", groups)
    *there, far_last = together(*there, far_last)

    here = [jnp.concatenate(spread(after(at(h), there[-1]), "seq", groups))]
    there = spread(jnp.concatenate(there), "tp", tp_parts)
    out_pair = jnp.stack([w_out, jnp.concatenate([far_first, far_last])])
    theirs_vk, mine_q, out_pair, *both = together(theirs_vk, mine_q, out_pair, *there, *here)
    there, here = both[:tp_parts], both[tp_parts:]

    weights_vk = weight_of(mine_vk, theirs_vk)
    there_vk = partial_sums(there, weights_vk)
    recv_vk = sent_over(there_vk)
    here = spread(here[0], "tp", tp_parts)
    theirs_q = flipped(after(mine_q, there_vk), "seq", low)
    here_vk = partial_sums(here, weights_vk)
    fast = tp_parts == 2 and groups == 4
    columns = []
    if fast:
        columns = [after(out_pair, here[-1])]
        columns = columns + [flipped(columns[0], "seq", off) for off in (1, 2)]
    recv_vk, theirs_q, here_vk, *columns = together(recv_vk, theirs_q, here_vk, *columns)

    def last_rows(value):
        end = ((groups - 1) ^ g) * rows + rows - HALO
        return lax.dynamic_slice_in_dim(value, end, HALO, 0).astype(F32)

    vk_halo = lax.ppermute(
        last_rows(here_vk) + last_rows(recv_vk), "seq", [(i, i + low) for i in range(seq_parts - low)]
    )

    weights_q = weight_of(mine_q, theirs_q)
    there_q = partial_sums(there, weights_q)
    recv_q = sent_over(there_q)
    here_q = partial_sums(here, weights_q)
    near_q, far_q = rows_before(here_q, there_q)

    def named(vk, q):
        shape = (groups, rows, width)
        return (vk[:, :width].reshape(shape), vk[:, width:].reshape(shape), q.reshape(shape))

    (here_v, here_k, here_q), (recv_v, recv_k, recv_q) = named(here_vk, here_q), named(recv_vk, recv_q)
    v_halo, k_halo = vk_halo[:, :width], vk_halo[:, width:]
    lanes = min(128, width)
    padded = pltpu.VMEM((HALO + length, lanes), F32)
    drive, entry, last = call_by_lanes(
        functools.partial(drive_kernel, groups, rows, order),
        lanes,
        (g_in, here_k, recv_k, k_halo, here_v, recv_v, v_halo, taps[1], taps[2], rates),
        (
            jax.ShapeDtypeStruct((length, width), F32),
            jax.ShapeDtypeStruct((SEGMENTS, order, width), F32),
            jax.ShapeDtypeStruct((order, width), F32),
        ),
        [padded, padded, pltpu.VMEM((order, SEGMENTS, lanes), F32)],
        length * width * (2 * order + 16),
    )
    fade = jnp.exp(-rates * float(length))
    beside = flipped(jnp.concatenate([last, near_q, far_q]), "seq", low)
    beside, near_q, far_q = beside[:order], beside[order : order + HALO], beside[order + HALO :]
    ended = jnp.where(l == 0, last * fade + beside, beside * fade + last)
    across = flipped(jnp.concatenate([ended, far_q]), "seq", high)
    across, far_q = across[:order], across[order:]
    before = jnp.where(h == 1, across * jnp.where(l == 1, fade, 1.0), 0.0)
    before = before + jnp.where(l == 1, beside, 0.0)
    q_halo = halo_of(near_q, far_q)
    if fast:
        across_own = flipped(columns[1][0], "seq", 2)
        across_far = flipped(columns[2][1], "seq", 1)
        own_columns, far_columns = (
            jnp.concatenate(in_order([columns[0][i], columns[1][i], columns[2][i], last_block], g), axis=1)
            for i, last_block in enumerate((across_own, across_far))
        )
        keep_columns = jnp.where(h == core, own_columns, far_columns)
        give_columns = jnp.where(h == core, far_columns, own_columns)
        before, keep_columns, give_columns = together(before, keep_columns, give_columns)
    (gated,) = call_by_lanes(
        functools.partial(gate_kernel, groups, rows, order),
        lanes,
        (g_in, drive, entry, before, here_q, recv_q, q_halo, taps[0], rates, heights, skip),
        (jax.ShapeDtypeStruct((length, width), BF16),),
        [
            padded,
            pltpu.VMEM((SEGMENTS, order, lanes), F32),
            pltpu.VMEM((length, lanes), F32),
        ],
        length * width * (4 * order + 16),
    )
    gated = gated.reshape(groups, rows, width)
    if not fast:
        mine = swapped(gated, layers).transpose(1, 0, 2).reshape(rows, groups * width)
        columns = lax.all_gather(w_out, "seq", axis=1, tiled=True)
        partial_out = dot(mine, columns).astype(BF16)
        return lax.psum_scatter(partial_out, "tp", scatter_dimension=1, tiled=True)
    both = swapped(jnp.concatenate([gated, gated]), halves)
    both = both.reshape(2, groups, rows, width).transpose(0, 2, 1, 3)
    both = both.reshape(2 * rows, groups * width)
    give = dot(both, give_columns).astype(BF16)
    keep = dot(both, keep_columns)
    summed = (keep + flipped(give, "tp", 1).astype(F32)).astype(BF16)
    summed = summed.reshape(2, rows, -1)
    ours = lax.dynamic_index_in_dim(summed, l, 0, False)
    theirs = flipped(lax.dynamic_index_in_dim(summed, 1 - l, 0, False), "seq", low)
    return jnp.where(
        l == 0,
        jnp.concatenate([ours, theirs], axis=1),
        jnp.concatenate([theirs, ours], axis=1),
    )


def solution(mesh):
    in_specs = (
        P("seq", None),
        P("seq", "tp"),
        P("seq", "tp"),
        P("seq", "tp"),
        P(None, None, "tp"),
        P(None, "tp"),
        P(None, "tp"),
        P("tp"),
        P("tp", "seq"),
    )
    out_specs = P("seq", "tp")
    return jax.shard_map(body, mesh=mesh, in_specs=in_specs, out_specs=out_specs, check_vma=False)
```

```python
import functools

import jax
import jax.numpy as jnp
from jax import lax
from jax.experimental import pallas as pl
from jax.experimental.pallas import tpu as pltpu
from jax.sharding import PartitionSpec as P

SHORT = 3
HALO = 8
SEGMENTS = 8
BF16 = jnp.bfloat16
F32 = jnp.float32


def flipped(value, axis, mask):
    size = lax.axis_size(axis)
    return lax.ppermute(value, axis, [(i, i ^ mask) for i in range(size)])


def spread(value, axis, count):
    return [value] + [flipped(value, axis, off) for off in range(1, count)]


def swapped(blocks, groups):
    return lax.all_to_all(blocks, "seq", 0, 0, axis_index_groups=groups)


def after(value, *others):
    return lax.optimization_barrier((value, *others))[0]


def together(*values):
    return lax.optimization_barrier(values)


def in_order(blocks, g):
    count = len(blocks)
    ordered = []
    for n in range(count):
        block = blocks[n]
        for value in range(1, count):
            block = jnp.where(g == value, blocks[n ^ value], block)
        ordered.append(block)
    return ordered


def dot(left, right):
    return jnp.dot(left, right, preferred_element_type=F32)


def load_projected(g, padded, own, recv, halo, groups, rows):
    padded[0:HALO, :] = halo[...]
    for block in range(groups):
        source = lax.bitwise_xor(g, jnp.int32(block))
        start = HALO + block * rows
        padded[start : start + rows, :] = own[source] + recv[source].astype(F32)


def short_filter(padded, taps, start, rows):
    total = taps[0:1, :] * padded[HALO + start : HALO + start + rows, :]
    for lag in range(1, SHORT):
        first = HALO + start - lag
        total = total + taps[lag : lag + 1, :] * padded[first : first + rows, :]
    return total


def drive_kernel(
    groups, rows, order,
    g_ref, k_own, k_recv, k_halo, v_own, v_recv, v_halo, k_taps, v_taps, rates,
    drive, entry, last, k_pad, v_pad, ends,
):
    g = g_ref[0]
    load_projected(g, k_pad, k_own, k_recv, k_halo, groups, rows)
    load_projected(g, v_pad, v_own, v_recv, v_halo, groups, rows)
    length = groups * rows
    step_rows = min(64, rows)
    for start in range(0, length, step_rows):
        drive[start : start + step_rows, :] = short_filter(
            k_pad, k_taps, start, step_rows
        ) * short_filter(v_pad, v_taps, start, step_rows)
    segment = length // SEGMENTS
    lanes = drive.shape[1]
    factors = jnp.exp(-rates[...])
    wide = [jnp.broadcast_to(factors[j : j + 1, :], (SEGMENTS, lanes)) for j in range(order)]

    def step(t, states):
        now = drive[pl.ds(t, SEGMENTS, stride=segment), :]
        return tuple(s * f + now for s, f in zip(states, wide))

    zero = jnp.zeros((SEGMENTS, lanes), F32)
    states = lax.fori_loop(0, segment, step, (zero,) * order, unroll=8)
    for j in range(order):
        ends[j] = states[j]
    whole = jnp.exp(-rates[...] * float(segment))
    running = jnp.zeros((order, lanes), F32)
    for i in range(SEGMENTS):
        entry[i] = running
        running = running * whole + ends[:, i, :]
    last[...] = running


def gate_kernel(
    groups, rows, order,
    g_ref, drive, entry, before, q_own, q_recv, q_halo, q_taps, rates, residues, skip,
    gated, q_pad, begin, response,
):
    g = g_ref[0]
    length = groups * rows
    segment = length // SEGMENTS
    lanes = drive.shape[1]
    decay = rates[...]
    for i in range(SEGMENTS):
        begin[i] = entry[i] + jnp.exp(-decay * float(segment * i)) * before[...]
    factors = jnp.exp(-decay)
    weights = residues[...]
    wide = [jnp.broadcast_to(factors[j : j + 1, :], (SEGMENTS, lanes)) for j in range(order)]
    heavy = [jnp.broadcast_to(weights[j : j + 1, :], (SEGMENTS, lanes)) for j in range(order)]
    direct = jnp.broadcast_to(skip[...], (SEGMENTS, lanes))

    def step(t, states):
        now = drive[pl.ds(t, SEGMENTS, stride=segment), :]
        states = tuple(s * f + now for s, f in zip(states, wide))
        terms = [s * w for s, w in zip(states, heavy)] + [direct * now]
        while len(terms) > 1:
            terms = [sum(terms[i : i + 2]) for i in range(0, len(terms), 2)]
        response[pl.ds(t, SEGMENTS, stride=segment), :] = terms[0]
        return states

    first = tuple(begin[:, j, :] for j in range(order))
    lax.fori_loop(0, segment, step, first, unroll=4)
    load_projected(g, q_pad, q_own, q_recv, q_halo, groups, rows)
    step_rows = min(64, rows)
    for start in range(0, length, step_rows):
        value = short_filter(q_pad, q_taps, start, step_rows) * response[start : start + step_rows, :]
        gated[start : start + step_rows, :] = value.astype(BF16)


def assemble_kernel(depth, cuts, place, *refs):
    count = len(refs) - len(cuts)
    for off in range(count):
        start = pl.multiple_of(lax.bitwise_xor(place[0], jnp.int32(off)) * depth, depth)
        for (first, last), out in zip(cuts, refs[count:]):
            out[pl.ds(start, depth), :] = refs[off][:, first:last]


def assemble(place, blocks, cuts):
    depth = blocks[0].shape[0]
    outs = [jax.ShapeDtypeStruct((len(blocks) * depth, last - first), BF16) for first, last in cuts]
    return pl.pallas_call(
        functools.partial(assemble_kernel, depth, cuts),
        in_specs=[pl.BlockSpec(memory_space=pltpu.SMEM)]
        + [pl.BlockSpec(memory_space=pltpu.VMEM)] * len(blocks),
        out_specs=[pl.BlockSpec(memory_space=pltpu.VMEM)] * len(outs),
        out_shape=outs,
        compiler_params=pltpu.CompilerParams(vmem_limit_bytes=32 * 1024 * 1024),
        cost_estimate=pl.CostEstimate(
            flops=0, bytes_accessed=sum(a.size * 2 for a in [*blocks, *outs]), transcendentals=0
        ),
    )(place, *blocks)


def by_lanes(shape, lanes):
    lead = len(shape) - 1
    return pl.BlockSpec((*shape[:-1], lanes), lambda i: (0,) * lead + (i,))


def call_by_lanes(kernel, lanes, args, outs, scratch, flops):
    width = outs[0].shape[-1]
    specs = [pl.BlockSpec(memory_space=pltpu.SMEM)] + [by_lanes(a.shape, lanes) for a in args[1:]]
    moved = sum(a.size * a.dtype.itemsize for a in [*args, *outs])
    return pl.pallas_call(
        kernel,
        grid=(width // lanes,),
        in_specs=specs,
        out_specs=[by_lanes(o.shape, lanes) for o in outs],
        out_shape=outs,
        scratch_shapes=scratch,
        compiler_params=pltpu.CompilerParams(vmem_limit_bytes=32 * 1024 * 1024),
        cost_estimate=pl.CostEstimate(flops=flops, bytes_accessed=moved, transcendentals=0),
    )(*args)


def body(tokens, w_query, w_key, w_value, short_taps, decay_rates, residues, skip_gain, w_out):
    seq_parts, tp_parts = lax.axis_size("seq"), lax.axis_size("tp")
    me, core = lax.axis_index("seq"), lax.axis_index("tp")
    rows, depth = tokens.shape
    order = decay_rates.shape[0]
    groups = seq_parts // 4
    low, high = groups, 2 * groups
    h, l, g = me // high, me // low % 2, me % groups
    width = w_query.shape[1] // groups
    half = depth // 2
    share = half // tp_parts
    length = groups * rows
    layers = [[layer * groups + i for i in range(groups)] for layer in range(4)]
    halves = [[side * high + i for i in range(high)] for side in range(2)]
    g_in = g.astype(jnp.int32).reshape(1)

    def at(side):
        return lax.dynamic_slice(tokens, (0, side * half + core * share), (rows, share))

    def block_of(w, off):
        return lax.dynamic_slice_in_dim(w, (g ^ off) * width, width, 1)

    def channels(value):
        return lax.dynamic_slice_in_dim(value, g * width, width, value.ndim - 1)

    def weight_of(mine, theirs):
        if tp_parts == 2:
            return [jnp.where((core ^ off) == l, mine, theirs) for off in range(2)]
        both = jnp.where(
            l == 0, jnp.concatenate([mine, theirs]), jnp.concatenate([theirs, mine])
        )
        return [
            lax.dynamic_slice(both, ((core ^ off) * share, 0), (share, mine.shape[1]))
            for off in range(tp_parts)
        ]

    def partial_sums(shares, weights):
        return sum(dot(t, w) for t, w in zip(shares, weights))

    def sent_over(value):
        return flipped(value.astype(BF16), "seq", high)

    def rows_before(mine, theirs):
        last = (groups - 1) ^ g

        def tail(value):
            value = value.reshape(groups, rows, -1)
            return lax.dynamic_index_in_dim(value, last, 0, False)[rows - HALO :]

        mine, theirs = tail(mine), tail(theirs)
        return jnp.where(l == 0, mine, theirs), jnp.where(l == 0, theirs, mine)

    def halo_of(near, far):
        return jnp.where((h == 0) & (l == 0), 0.0, near + far)

    given = at(1 - h)
    got = flipped(given, "seq", high)
    all_weights = [after(w, given) for w in (w_value, w_key, w_query)]
    flat = together(
        *(
            jnp.concatenate([block_of(w, off) for w in all_weights], axis=1)
            for off in range(groups)
        )
    )
    came = [flat[0]] + [flipped(flat[off], "seq", off) for off in range(1, groups)]
    out_depth = w_out.shape[0] // 2
    far_first = flipped(w_out[:out_depth], "seq", high)
    got, far_first, taps, rates, heights, skip, *came = together(
        got, far_first, channels(short_taps), channels(decay_rates), channels(residues),
        channels(skip_gain[None, :]), *came,
    )
    cuts = ((0, 2 * width), (2 * width, 3 * width))
    if width % 128 == 0 and w_query.shape[0] % 16 == 0:
        mine_vk, mine_q = assemble(g_in, came, cuts)
    else:
        whole = jnp.concatenate(in_order(came, g))
        mine_vk, mine_q = (whole[:, first:last] for first, last in cuts)

    theirs_vk = flipped(mine_vk, "seq", low)
    far_last = flipped(after(w_out[out_depth:], got), "seq", high)
    there = spread(got, "seq", groups)
    *there, far_last = together(*there, far_last)

    here = [jnp.concatenate(spread(after(at(h), there[-1]), "seq", groups))]
    there = spread(jnp.concatenate(there), "tp", tp_parts)
    out_pair = jnp.stack([w_out, jnp.concatenate([far_first, far_last])])
    theirs_vk, mine_q, out_pair, *both = together(theirs_vk, mine_q, out_pair, *there, *here)
    there, here = both[:tp_parts], both[tp_parts:]

    weights_vk = weight_of(mine_vk, theirs_vk)
    there_vk = partial_sums(there, weights_vk)
    recv_vk = sent_over(there_vk)
    here = spread(here[0], "tp", tp_parts)
    theirs_q = flipped(after(mine_q, there_vk), "seq", low)
    here_vk = partial_sums(here, weights_vk)
    fast = tp_parts == 2 and groups == 4
    columns = []
    if fast:
        columns = [out_pair]
        columns = columns + [flipped(columns[0], "seq", off) for off in (1, 2)]
    recv_vk, theirs_q, here_vk, *columns = together(recv_vk, theirs_q, here_vk, *columns)

    def last_rows(value):
        end = ((groups - 1) ^ g) * rows + rows - HALO
        return lax.dynamic_slice_in_dim(value, end, HALO, 0).astype(F32)

    vk_halo = lax.ppermute(
        last_rows(here_vk) + last_rows(recv_vk), "seq", [(i, i + low) for i in range(seq_parts - low)]
    )

    weights_q = weight_of(mine_q, theirs_q)
    there_q = partial_sums(there, weights_q)
    recv_q = sent_over(there_q)
    here_q = partial_sums(here, weights_q)
    near_q, far_q = rows_before(here_q, there_q)

    def named(vk, q):
        shape = (groups, rows, width)
        return (vk[:, :width].reshape(shape), vk[:, width:].reshape(shape), q.reshape(shape))

    (here_v, here_k, here_q), (recv_v, recv_k, recv_q) = named(here_vk, here_q), named(recv_vk, recv_q)
    v_halo, k_halo = vk_halo[:, :width], vk_halo[:, width:]
    lanes = min(128, width)
    padded = pltpu.VMEM((HALO + length, lanes), F32)
    drive, entry, last = call_by_lanes(
        functools.partial(drive_kernel, groups, rows, order),
        lanes,
        (g_in, here_k, recv_k, k_halo, here_v, recv_v, v_halo, taps[1], taps[2], rates),
        (
            jax.ShapeDtypeStruct((length, width), F32),
            jax.ShapeDtypeStruct((SEGMENTS, order, width), F32),
            jax.ShapeDtypeStruct((order, width), F32),
        ),
        [padded, padded, pltpu.VMEM((order, SEGMENTS, lanes), F32)],
        length * width * (2 * order + 16),
    )
    fade = jnp.exp(-rates * float(length))
    beside = flipped(jnp.concatenate([last, near_q, far_q]), "seq", low)
    beside, near_q, far_q = beside[:order], beside[order : order + HALO], beside[order + HALO :]
    ended = jnp.where(l == 0, last * fade + beside, beside * fade + last)
    across = flipped(jnp.concatenate([ended, far_q]), "seq", high)
    across, far_q = across[:order], across[order:]
    before = jnp.where(h == 1, across * jnp.where(l == 1, fade, 1.0), 0.0)
    before = before + jnp.where(l == 1, beside, 0.0)
    q_halo = halo_of(near_q, far_q)
    if fast:
        across_own = flipped(columns[1][0], "seq", 2)
        across_far = flipped(columns[2][1], "seq", 1)
        own_columns, far_columns = (
            jnp.concatenate(in_order([columns[0][i], columns[1][i], columns[2][i], last_block], g), axis=1)
            for i, last_block in enumerate((across_own, across_far))
        )
        keep_columns = jnp.where(h == core, own_columns, far_columns)
        give_columns = jnp.where(h == core, far_columns, own_columns)
        before, keep_columns, give_columns = together(before, keep_columns, give_columns)
    (gated,) = call_by_lanes(
        functools.partial(gate_kernel, groups, rows, order),
        lanes,
        (g_in, drive, entry, before, here_q, recv_q, q_halo, taps[0], rates, heights, skip),
        (jax.ShapeDtypeStruct((length, width), BF16),),
        [
            padded,
            pltpu.VMEM((SEGMENTS, order, lanes), F32),
            pltpu.VMEM((length, lanes), F32),
        ],
        length * width * (4 * order + 16),
    )
    gated = gated.reshape(groups, rows, width)
    if not fast:
        mine = swapped(gated, layers).transpose(1, 0, 2).reshape(rows, groups * width)
        columns = lax.all_gather(w_out, "seq", axis=1, tiled=True)
        partial_out = dot(mine, columns).astype(BF16)
        return lax.psum_scatter(partial_out, "tp", scatter_dimension=1, tiled=True)
    both = swapped(jnp.concatenate([gated, gated]), halves)
    both = both.reshape(2, groups, rows, width).transpose(0, 2, 1, 3)
    both = both.reshape(2 * rows, groups * width)
    give = dot(both, give_columns).astype(BF16)
    keep = dot(both, keep_columns)
    summed = (keep + flipped(give, "tp", 1).astype(F32)).astype(BF16)
    summed = summed.reshape(2, rows, -1)
    ours = lax.dynamic_index_in_dim(summed, l, 0, False)
    theirs = flipped(lax.dynamic_index_in_dim(summed, 1 - l, 0, False), "seq", low)
    return jnp.where(
        l == 0,
        jnp.concatenate([ours, theirs], axis=1),
        jnp.concatenate([theirs, ours], axis=1),
    )


def solution(mesh):
    in_specs = (
        P("seq", None),
        P("seq", "tp"),
        P("seq", "tp"),
        P("seq", "tp"),
        P(None, None, "tp"),
        P(None, "tp"),
        P(None, "tp"),
        P("tp"),
        P("tp", "seq"),
    )
    out_specs = P("seq", "tp")
    return jax.shard_map(body, mesh=mesh, in_specs=in_specs, out_specs=out_specs, check_vma=False)
```
